256 devices in a mesh: seq: 64 (over x, z_lo, y), fsdp: 4 (over z_hi, core).
Axes of the slice: x: 4, y: 4, z: 8 (z_hi: 2, z_lo: 4; z = z_hi * 4 + z_lo), core: 2. Of those that a mesh axis runs over, the one named last changes fastest.
Arguments:
- hidden: bfloat16 [65536, 3584], P(('seq', 'fsdp')), may hold values from -6 to 6
- queries: bfloat16 [65536, 2048], P(('seq', 'fsdp')), may hold values from -360 to 360
- kv_weights: bfloat16 [2, 3584, 1024], P(None, 'fsdp'), may hold values from -0.09375 to 0.09375
- image_groups: int32 [64], P('seq'), may hold values 0 or 1
- doc_ids: int32 [65536], replicated, may hold values from 0 to 63, never falling along the last dimension, each value on 1 to 3072 neighbouring positions
Outputs:
- attended: bfloat16 [65536, 2048], P(('seq', 'fsdp'))
The draws below stay inside these ranges and needn't reach their ends.
Inputs may be any that keep to these rules, and one draw needn't show every extreme that they name: `image_groups`: 1 marks a group of image tokens. `doc_ids`: never falling along the tokens; every document has 1 to 3072 tokens and one has exactly that many.
All inputs are finite; a program needn't handle non-finite values.
Results may differ from the reference program's by a relative error of at most 0.0055.
The reference program's roundings to bfloat16 on the way (of `keys_values` and `weights`) count: a program that leaves them out, or rounds other values in their place, can miss the bound.
Values may be sent and summed in bfloat16 or wider, within the bound.
No kernel may reach another device: no remote copies, remote signals or barrier semaphores. Data moves between devices by JAX's collectives and lax.ppermute only.
A program may use at most 128 MiB of HBM per device.

```python
import math
import jax
import jax.numpy as jnp
import numpy as np
from jax import lax

D = 3584
KVH = 4
HD = 128
QH = 16
ROWS = 256
SPAN = 3
TOKENS = 65536
DOCS = 64
N_SEQ = 64
N_FSDP = 4


def draw_queries(key, part):
    base = jnp.clip(jax.random.normal(key, (TOKENS, QH * HD), jnp.float32), -6.0, 6.0)
    return base.astype(jnp.bfloat16)


def set_ends(array, own_key, smallest, high):
    index_at = [jax.random.randint(jax.random.fold_in(own_key, axis), (), 0, length) for axis, length in enumerate(array.shape)]
    longest = array.shape.index(max(array.shape))
    neighbour = index_at[:longest] + [(index_at[longest] + 1) % array.shape[longest]] + index_at[longest + 1:]
    return array.at[tuple(index_at)].set(smallest).at[tuple(neighbour)].set(high)


def levels(key, extent, cuts, smallest, top_value):
    loudness, own = 1.0, jax.random.fold_in(key, 6)
    for axis_at, shards_of in cuts:
        heights = jnp.exp(jax.random.uniform(jax.random.fold_in(own, axis_at), (shards_of,), jnp.float32, smallest / len(cuts), top_value / len(cuts)))
        loudness = loudness * jnp.repeat(heights, extent[axis_at] // shards_of).reshape([-1 if axis == axis_at else 1 for axis in range(len(extent))])
    return loudness


def profile(count, total, most, slope):
    loads = [(1 << 20) // math.isqrt(rank ** slope) + 1 for rank in range(2, count + 1)]
    surplus, given = total - most - (count - 1), [1] * (count - 1)
    while surplus > 0:
        movable = [i for i in range(count - 1) if given[i] < most]
        pool, budget = sum([loads[i] for i in movable]), surplus
        for i in movable:
            more = min(most - given[i], max(1, budget * loads[i] // pool), surplus)
            given[i] = given[i] + more
            surplus = surplus - more
    return np.array([most] + given)


def uneven_parts(rng, number_of, total, bound, skew):
    if number_of == 2:
        one = jax.random.randint(rng, (), max(1, total - bound), min(bound, total - 1) + 1)
        return jnp.stack([one, total - one])
    tallies = jnp.asarray(profile(number_of, total, bound, skew), jnp.int32)
    couples = (number_of - 1) // 2
    donor, sink = tallies[1:1 + 2 * couples:2], tallies[2:2 + 2 * couples:2]
    margin = jnp.minimum(donor - 1, bound - sink)
    passed = jax.random.randint(jax.random.fold_in(rng, 1), (couples,), 0, 1 << 20) % (margin + 1)
    tallies = tallies.at[1:1 + 2 * couples:2].set(donor - passed).at[2:2 + 2 * couples:2].set(sink + passed)
    return tallies[jax.random.permutation(jax.random.fold_in(rng, 2), number_of)]


def centred(rng, extent, deviation, most, pieces=(), kind=jnp.bfloat16):
    drawn = deviation * jax.random.normal(rng, extent, jnp.float32)
    if pieces:
        drawn = drawn * levels(rng, extent, pieces, -0.22, 0.18)
    return jnp.clip(drawn, -most, most).astype(kind)


def setup_inputs(seed: int = 0) -> dict:
    keys = jax.random.split(jax.random.key(seed), 6)
    hidden = centred(keys[0], (TOKENS, D), 1.0, 6.0, ((0, 256),))
    queries = draw_queries(jax.random.fold_in(keys[5], 71), 0)
    kv_weights = centred(keys[2], (2, D, 2 * KVH * HD), D ** -0.5, 0.09375, ((1, 4),))
    image_groups = set_ends((jax.random.randint(keys[3], (N_SEQ,), 0, 3) < 1).astype(jnp.int32), jax.random.fold_in(keys[3], 1), 0, 1)
    doc_ids = jnp.searchsorted(jnp.cumsum(uneven_parts(keys[4], DOCS, TOKENS, SPAN * ROWS * N_FSDP, 2)), jnp.arange(TOKENS), side="right").astype(jnp.int32)
    return {"hidden": hidden, "queries": queries, "kv_weights": kv_weights, "image_groups": image_groups, "doc_ids": doc_ids}


def build_mask(query_pos, key_pos, doc_ids, is_image, own_start):
    key_doc = jnp.where(key_pos >= 0, doc_ids[jnp.maximum(key_pos, 0)], -1)
    query_doc = doc_ids[query_pos]
    same_doc = query_doc[:, None] == key_doc[None, :]
    earlier = key_pos[None, :] <= query_pos[:, None]
    own_image = jnp.logical_and(is_image, key_pos[None, :] >= own_start)
    return jnp.logical_and(same_doc, jnp.logical_or(earlier, own_image))

def attend(query_rows, keys_values, allowed):
    n_query = query_rows.shape[0]
    n_keys = keys_values.shape[0]
    per_group = QH // KVH
    score_scale = 1.0 / math.sqrt(HD)
    query_heads = query_rows.reshape(n_query, KVH, per_group, HD).transpose(1, 0, 2, 3)
    key_heads = keys_values[:, :KVH * HD].reshape(n_keys, KVH, HD).transpose(1, 0, 2)
    value_heads = keys_values[:, KVH * HD:].reshape(n_keys, KVH, HD).transpose(1, 0, 2)

    def one_head(operands):
        head_q, head_k, head_v = operands
        scores = jnp.einsum('rgd,kd->grk', head_q.astype(jnp.float32), head_k.astype(jnp.float32)) * score_scale
        scores = jnp.where(allowed[None], scores, -1e+30)
        highest = lax.optimization_barrier(jnp.max(scores, axis=-1, keepdims=True))
        weights = jnp.where(allowed[None], jnp.exp(scores - highest), 0.0)
        totals = lax.optimization_barrier(jnp.sum(weights, axis=-1))
        rounded = lax.optimization_barrier(weights.astype(jnp.bfloat16))
        summed = jnp.einsum('grk,kd->rgd', rounded.astype(jnp.float32), head_v.astype(jnp.float32))
        return (summed / jnp.transpose(totals)[:, :, None]).astype(jnp.bfloat16)
    mixed = lax.map(one_head, (query_heads, key_heads, value_heads))
    return mixed.transpose(1, 0, 2, 3).reshape(n_query, QH * HD)

def reference(hidden, queries, kv_weights, image_groups, doc_ids):
    block_len = TOKENS // N_SEQ
    kv_width = 2 * KVH * HD

    def project(group):
        block_hidden = lax.dynamic_slice_in_dim(hidden, group * block_len, block_len, 0)
        weight = lax.dynamic_index_in_dim(kv_weights, image_groups[group], 0, keepdims=False)
        return jnp.dot(block_hidden, weight, preferred_element_type=jnp.float32).astype(jnp.bfloat16)
    kv_blocks = lax.map(project, jnp.arange(N_SEQ, dtype=jnp.int32))
    padded = jnp.concatenate([jnp.zeros((SPAN, block_len, kv_width), kv_blocks.dtype), kv_blocks], 0)

    def one_block(group):
        query_rows = lax.dynamic_slice_in_dim(queries, group * block_len, block_len, 0)
        window = lax.dynamic_slice_in_dim(padded, group, SPAN + 1, 0).reshape((SPAN + 1) * block_len, kv_width)
        offsets = group - SPAN + jnp.arange(SPAN + 1, dtype=jnp.int32)
        key_pos = (offsets[:, None] * block_len + jnp.arange(block_len, dtype=jnp.int32)[None, :]).reshape(-1)
        query_pos = group * block_len + jnp.arange(block_len, dtype=jnp.int32)
        allowed = build_mask(query_pos, key_pos, doc_ids, image_groups[group] == 1, group * block_len)
        return attend(query_rows, window, allowed)
    attended = lax.map(one_block, jnp.arange(N_SEQ, dtype=jnp.int32))
    return attended.reshape(TOKENS, QH * HD)
```

```python
import functools
import math

import jax
import jax.numpy as jnp
from jax import lax
from jax.experimental import pallas as pl
from jax.experimental.pallas import tpu as pltpu
from jax.sharding import PartitionSpec as P

KVH = 4
HD = 128
QH = 16
SPAN = 3
N_FSDP = 4
GROUP = QH // KVH
CORE_HEADS = KVH // 2
CHUNKS = 2
CHUNK_HEADS = CORE_HEADS // CHUNKS
TQ = 128
TK = 512
FLAT = ("seq", "fsdp")
NEG = -1e30


def swap(block, bits, n_seq):
    route = [(s * N_FSDP + f, s * N_FSDP + (f ^ bits)) for s in range(n_seq) for f in range(N_FSDP)]
    return lax.ppermute(block, FLAT, route)


def from_behind(block, distance, n_seq):
    route = [
        (s * N_FSDP + f, (s + distance) * N_FSDP + f)
        for s in range(n_seq - distance)
        for f in range(N_FSDP)
    ]
    return lax.ppermute(block, FLAT, route)


def pick_kernel(at, w_ref, *rest):
    outs, sems = rest[:-1], rest[-1]
    copies = []
    width = CHUNK_HEADS * HD
    for chunk in range(CHUNKS):
        for side in range(2):
            core = at[1] if side == 0 else 1 - at[1]
            for part in range(2):
                column = part * KVH * HD + core * (CORE_HEADS * HD) + chunk * width
                copies.append(
                    pltpu.make_async_copy(
                        w_ref.at[at[0], :, pl.ds(pl.multiple_of(column, 128), width)],
                        outs[chunk * 2 + side].at[:, pl.ds(part * width, width)],
                        sems.at[len(copies)],
                    )
                )
    for copy in copies:
        copy.start()
    for copy in copies:
        copy.wait()


def pick(modality, core, kv_weights):
    depth = kv_weights.shape[1]
    shape = jax.ShapeDtypeStruct((depth, CHUNK_HEADS * 2 * HD), jnp.bfloat16)
    n = 2 * CHUNKS
    return pl.pallas_call(
        pick_kernel,
        out_shape=[shape] * n,
        grid_spec=pltpu.PrefetchScalarGridSpec(
            num_scalar_prefetch=1,
            grid=(1,),
            in_specs=[pl.BlockSpec(memory_space=pl.ANY)],
            out_specs=[pl.BlockSpec(memory_space=pl.ANY)] * n,
            scratch_shapes=[pltpu.SemaphoreType.DMA((2 * n,))],
        ),
        name="pick_weights",
    )(jnp.stack([modality, core]), kv_weights)


def project_kernel(at, own_a, own_b, par_a, par_b, wa, wb, *rest, has_acc):
    acc, out = rest if has_acc else (None, rest[0])
    rows = own_a.shape[0]
    for mine, (xa, xb) in enumerate(((par_a, par_b), (own_a, own_b))):
        start = pl.multiple_of((at[0] if mine else 1 - at[0]) * rows, rows)
        total = jnp.dot(xa[...], wa[...], preferred_element_type=jnp.float32)
        total += jnp.dot(xb[...], wb[...], preferred_element_type=jnp.float32)
        if has_acc:
            total += acc[pl.ds(start, rows), :]
        out[pl.ds(start, rows), :] = total.astype(out.dtype)


def project(core, part_a, part_b, hidden, partner, wa, wb, acc):
    rows, depth, width = hidden.shape[0], wa.shape[0], wa.shape[1]
    has_acc = acc is not None
    whole = lambda i, at: (0, 0)
    in_specs = [
        pl.BlockSpec((rows, depth), lambda i, at: (0, at[1])),
        pl.BlockSpec((rows, depth), lambda i, at: (0, at[2])),
        pl.BlockSpec((rows, depth), lambda i, at: (0, at[1])),
        pl.BlockSpec((rows, depth), lambda i, at: (0, at[2])),
        pl.BlockSpec((depth, width), whole),
        pl.BlockSpec((depth, width), whole),
    ]
    args = [jnp.stack([core, part_a, part_b]), hidden, hidden, partner, partner, wa, wb]
    if has_acc:
        in_specs.append(pl.BlockSpec((2 * rows, width), whole))
        args.append(acc)
    return pl.pallas_call(
        functools.partial(project_kernel, has_acc=has_acc),
        out_shape=jax.ShapeDtypeStruct((2 * rows, width), jnp.bfloat16 if has_acc else jnp.float32),
        grid_spec=pltpu.PrefetchScalarGridSpec(
            num_scalar_prefetch=1,
            grid=(1,),
            in_specs=in_specs,
            out_specs=pl.BlockSpec((2 * rows, width), whole),
        ),
        compiler_params=pltpu.CompilerParams(vmem_limit_bytes=40 * 1024 * 1024),
        cost_estimate=pl.CostEstimate(
            flops=8 * rows * depth * width, bytes_accessed=8 * rows * depth + 4 * depth * width, transcendentals=0
        ),
        name="project_second" if has_acc else "project_first",
    )(*args)


def attend_kernel(at, q_own, q_par, query_doc, last_key, key_doc, *rest):
    windows, (out_own, out_par, keys, values, scores, sems) = rest[: SPAN + 1], rest[SPAN + 1 :]
    tile = pl.program_id(0)
    tiles = pl.num_programs(0)
    block_rows = windows[0].shape[0]
    width = CHUNK_HEADS * HD

    @pl.when(tile == 0)
    def _():
        copies = []
        for back in range(SPAN + 1):
            place = pl.ds((SPAN - back) * block_rows, block_rows)
            for part, held in enumerate((keys, values)):
                copies.append(
                    pltpu.make_async_copy(
                        windows[back].at[:, pl.ds(part * width, width)], held.at[place, :], sems.at[len(copies)]
                    )
                )
        for copy in copies:
            copy.start()
        for copy in copies:
            copy.wait()

    first, end = at[tile], at[tiles + tile]
    factor = math.log2(math.e) / math.sqrt(HD)
    for head in range(CHUNK_HEADS):
        lanes = slice(head * HD, (head + 1) * HD)

        def score(block, peaks):
            start = pl.multiple_of(block * TK, TK)
            place = pl.ds(start, TK)
            key = keys[place, lanes]
            position = start + lax.broadcasted_iota(jnp.int32, (TQ, TK), 1)
            allowed = jnp.logical_and(query_doc[...] == key_doc[:, place], position <= last_key[...])
            found = []
            for i in range(GROUP):
                columns = slice((head * GROUP + i) * HD, (head * GROUP + i + 1) * HD)
                query = jnp.where(tile < tiles // 2, q_own[:, columns], q_par[:, columns])
                s = lax.dot_general(query, key, (((1,), (1,)), ((), ())), preferred_element_type=jnp.float32)
                s = jnp.where(allowed, s, NEG)
                scores[i * TQ : (i + 1) * TQ, place] = s
                peak = peaks[i]
                for lane in range(0, TK, HD):
                    peak = jnp.maximum(peak, s[:, lane : lane + HD])
                found.append(peak)
            return tuple(found)

        start_peaks = tuple(jnp.full((TQ, HD), NEG, jnp.float32) for _ in range(GROUP))
        peaks = lax.fori_loop(first, end, score, start_peaks)
        highest = [jnp.max(peak, axis=1, keepdims=True) for peak in peaks]

        def weigh(block, carry):
            start = pl.multiple_of(block * TK, TK)
            place = pl.ds(start, TK)
            value = values[place, lanes]
            found = []
            for i in range(GROUP):
                total, summed = carry[i]
                w = jnp.exp2((scores[i * TQ : (i + 1) * TQ, place] - highest[i]) * factor)
                for lane in range(0, TK, HD):
                    total = total + w[:, lane : lane + HD]
                summed = summed + jnp.dot(w.astype(jnp.bfloat16), value, preferred_element_type=jnp.float32)
                found.append((total, summed))
            return tuple(found)

        zero = jnp.zeros((TQ, HD), jnp.float32)
        sums = lax.fori_loop(first, end, weigh, tuple((zero, zero) for _ in range(GROUP)))
        for i in range(GROUP):
            columns = slice((head * GROUP + i) * HD, (head * GROUP + i + 1) * HD)
            total, summed = sums[i]
            result = (summed / jnp.sum(total, axis=1, keepdims=True)).astype(jnp.bfloat16)

            @pl.when(tile < tiles // 2)
            def _():
                out_own[:, columns] = result

            @pl.when(tile >= tiles // 2)
            def _():
                out_par[:, columns] = result


def attend(at, q_own, q_par, query_doc, last_key, key_doc, windows, chunk):
    rows = q_own.shape[0]
    block_rows = windows[0].shape[0]
    n_keys = (SPAN + 1) * block_rows
    tiles = 2 * rows // TQ
    half = tiles // 2
    width = CHUNK_HEADS * GROUP * HD
    own = lambda i, at: (jnp.minimum(i, half - 1), 0)
    par = lambda i, at: (jnp.maximum(i - half, 0), 0)
    own_q = lambda i, at: (jnp.minimum(i, half - 1), chunk)
    par_q = lambda i, at: (jnp.maximum(i - half, 0), chunk)
    shape = jax.ShapeDtypeStruct((rows, width), jnp.bfloat16)
    return pl.pallas_call(
        attend_kernel,
        out_shape=[shape, shape],
        grid_spec=pltpu.PrefetchScalarGridSpec(
            num_scalar_prefetch=1,
            grid=(tiles,),
            in_specs=[
                pl.BlockSpec((TQ, width), own_q),
                pl.BlockSpec((TQ, width), par_q),
                pl.BlockSpec((TQ, 1), lambda i, at: (i, 0)),
                pl.BlockSpec((TQ, 1), lambda i, at: (i, 0)),
                pl.BlockSpec((1, n_keys), lambda i, at: (0, 0)),
            ]
            + [pl.BlockSpec(memory_space=pl.ANY)] * (SPAN + 1),
            out_specs=[pl.BlockSpec((TQ, width), own), pl.BlockSpec((TQ, width), par)],
            scratch_shapes=[
                pltpu.VMEM((n_keys, CHUNK_HEADS * HD), jnp.bfloat16),
                pltpu.VMEM((n_keys, CHUNK_HEADS * HD), jnp.bfloat16),
                pltpu.VMEM((GROUP * TQ, n_keys), jnp.float32),
                pltpu.SemaphoreType.DMA((2 * (SPAN + 1),)),
            ],
        ),
        compiler_params=pltpu.CompilerParams(vmem_limit_bytes=40 * 1024 * 1024),
        cost_estimate=pl.CostEstimate(
            flops=4 * 2 * rows * width * n_keys // 2, bytes_accessed=4 * n_keys * HD * CHUNK_HEADS, transcendentals=0
        ),
        name="attend",
    )(at, q_own, q_par, query_doc, last_key, key_doc, *windows)


def local(hidden, queries, kv_weights, image_groups, doc_ids):
    rows = hidden.shape[0]
    n_seq = lax.axis_size("seq")
    block_rows = rows * N_FSDP
    n_keys = (SPAN + 1) * block_rows
    seq_place = lax.axis_index("seq")
    fsdp_place = lax.axis_index("fsdp")
    core = fsdp_place % 2
    chip = fsdp_place // 2
    modality = image_groups[0]

    picked = pick(modality, core, kv_weights)
    mine, other = picked[0::2], picked[1::2]
    from_z = [swap(mine[j], 2, n_seq) for j in range(CHUNKS)]
    from_diagonal = [swap(other[j], 3, n_seq) for j in range(CHUNKS)]
    from_core = [swap(other[j], 1, n_seq) for j in range(CHUNKS)]
    partner = swap(hidden, 1, n_seq)
    half_heads = QH // 2 * HD
    q_own = lax.dynamic_slice_in_dim(queries, core * half_heads, half_heads, 1)
    q_par = swap(lax.dynamic_slice_in_dim(queries, (1 - core) * half_heads, half_heads, 1), 1, n_seq)

    padded = jnp.concatenate([jnp.full((SPAN * block_rows,), -1, jnp.int32), doc_ids])
    key_doc = lax.dynamic_slice_in_dim(padded, seq_place * block_rows, n_keys, 0)
    own_start = SPAN * block_rows + fsdp_place * rows
    par_start = SPAN * block_rows + (fsdp_place ^ 1) * rows
    starts = (own_start, par_start)
    query_doc = jnp.concatenate([lax.dynamic_slice_in_dim(key_doc, s, rows, 0) for s in starts])
    position = jnp.concatenate([s + jnp.arange(rows, dtype=jnp.int32) for s in starts])
    last_key = jnp.where(modality == 1, n_keys - 1, position)
    lowest = query_doc[::TQ]
    top = query_doc[TQ - 1 :: TQ]
    first = jnp.sum(key_doc[None, :] < lowest[:, None], axis=1) // TK
    doc_end = jnp.sum(key_doc[None, :] <= top[:, None], axis=1) - 1
    end = jnp.minimum(last_key[TQ - 1 :: TQ], doc_end) // TK + 1
    at = jnp.concatenate([first, end]).astype(jnp.int32)

    own_out, sent_out = [], []
    for j in range(CHUNKS):
        acc = project(core, fsdp_place, fsdp_place ^ 1, hidden, partner, mine[j], from_core[j], None)
        kv = project(core, fsdp_place ^ 2, fsdp_place ^ 3, hidden, partner, from_z[j], from_diagonal[j], acc)
        across = swap(kv, 2, n_seq)
        block_kv = jnp.where(chip == 0, jnp.concatenate([kv, across]), jnp.concatenate([across, kv]))
        windows = [block_kv] + [from_behind(block_kv, d, n_seq) for d in range(1, SPAN + 1)]
        out_own, out_par = attend(at, q_own, q_par, query_doc[:, None], last_key[:, None], key_doc[None, :], windows, j)
        own_out.append(out_own)
        sent_out.append(swap(out_par, 1, n_seq))
    own_out, sent_out = jnp.concatenate(own_out, 1), jnp.concatenate(sent_out, 1)
    return jnp.where(
        core == 0, jnp.concatenate([own_out, sent_out], 1), jnp.concatenate([sent_out, own_out], 1)
    )


def solution(mesh):
    in_specs = (
        P(("seq", "fsdp"), None),
        P(("seq", "fsdp"), None),
        P(None, "fsdp", None),
        P("seq"),
        P(),
    )
    out_specs = P(("seq", "fsdp"), None)
    return jax.shard_map(local, mesh=mesh, in_specs=in_specs, out_specs=out_specs, check_vma=False)
```

```python
import functools
import math

import jax
import jax.numpy as jnp
from jax import lax
from jax.experimental import pallas as pl
from jax.experimental.pallas import tpu as pltpu
from jax.sharding import PartitionSpec as P

KVH = 4
HD = 128
QH = 16
SPAN = 3
N_FSDP = 4
GROUP = QH // KVH
CORE_HEADS = KVH // 2
CHUNKS = 2
CHUNK_HEADS = CORE_HEADS // CHUNKS
RING = 4
TQ = 128
TK = 512
FLAT = ("seq", "fsdp")
NEG = -1e30


def swap(block, bits, n_seq):
    route = [(s * N_FSDP + f, s * N_FSDP + (f ^ bits)) for s in range(n_seq) for f in range(N_FSDP)]
    return lax.ppermute(block, FLAT, route)


def from_behind(block, distance, n_seq):
    route = [
        (s * N_FSDP + f, (s + distance) * N_FSDP + f)
        for s in range(n_seq - distance)
        for f in range(N_FSDP)
    ]
    return lax.ppermute(block, FLAT, route)


def along_x(block, distance, n_seq):
    step = n_seq // RING
    route = [
        (s * N_FSDP + f, (s + distance * step) % n_seq * N_FSDP + f)
        for s in range(n_seq)
        for f in range(N_FSDP)
    ]
    return lax.ppermute(block, FLAT, route)


def pick_kernel(at, w_ref, *outs):
    width = CHUNK_HEADS * HD
    for i in range(2 * CHUNKS):
        core = at[0] if i % 2 == 0 else 1 - at[0]
        for part in range(2):
            column = part * KVH * HD + core * (CORE_HEADS * HD) + i // 2 * width
            columns = pl.ds(pl.multiple_of(column, 128), width)
            outs[i][:, :, part * width : (part + 1) * width] = w_ref[:, :, columns]


def pick_own(core, modality, kv_weights):
    depth = kv_weights.shape[1]
    rows = depth // RING
    shape = (1, depth, CHUNK_HEADS * 2 * HD)
    n = 2 * CHUNKS
    return pl.pallas_call(
        pick_kernel,
        out_shape=[jax.ShapeDtypeStruct(shape, jnp.bfloat16)] * n,
        grid_spec=pltpu.PrefetchScalarGridSpec(
            num_scalar_prefetch=1,
            grid=(RING,),
            in_specs=[pl.BlockSpec((1, rows, kv_weights.shape[2]), lambda i, at: (at[1], i, 0))],
            out_specs=[pl.BlockSpec((1, rows, shape[2]), lambda i, at: (0, i, 0))] * n,
        ),
        name="pick_own",
    )(jnp.stack([core, modality]), kv_weights)


def pick_quarter(core, quarter, kv_weights):
    rows = kv_weights.shape[1] // RING
    shape = (2, rows, CHUNK_HEADS * 2 * HD)
    n = 2 * CHUNKS
    return pl.pallas_call(
        pick_kernel,
        out_shape=[jax.ShapeDtypeStruct(shape, jnp.bfloat16)] * n,
        grid_spec=pltpu.PrefetchScalarGridSpec(
            num_scalar_prefetch=1,
            grid=(1,),
            in_specs=[pl.BlockSpec((2, rows, kv_weights.shape[2]), lambda i, at: (0, at[1], 0))],
            out_specs=[pl.BlockSpec(shape, lambda i, at: (0, 0, 0))] * n,
        ),
        name="pick_quarter",
    )(jnp.stack([core, quarter]), kv_weights)


def piece_kernel(at, z_ref, d_ref, *outs):
    rows = z_ref.shape[1]
    for i, out in enumerate(outs):
        out[:rows, :] = z_ref[at[i]]
        out[rows:, :] = d_ref[at[i]]


def pieces(modalities, from_z, from_diagonal):
    shape = (2 * from_z.shape[1], from_z.shape[2])
    return pl.pallas_call(
        piece_kernel,
        out_shape=[jax.ShapeDtypeStruct(shape, jnp.bfloat16)] * RING,
        grid_spec=pltpu.PrefetchScalarGridSpec(
            num_scalar_prefetch=1,
            grid=(1,),
            in_specs=[pl.BlockSpec(from_z.shape, lambda i, at: (0, 0, 0))] * 2,
            out_specs=[pl.BlockSpec(shape, lambda i, at: (0, 0))] * RING,
        ),
        name="pieces",
    )(modalities, from_z, from_diagonal)


def project_rows(at, own, par, weights, acc, out):
    rows = out.shape[0] // 2
    for mine, x in enumerate((par, own)):
        start = pl.multiple_of((at[0] if mine else 1 - at[0]) * rows, rows)
        total = jnp.dot(x[0][...], weights[0][...], preferred_element_type=jnp.float32)
        total += jnp.dot(x[1][...], weights[1][...], preferred_element_type=jnp.float32)
        if acc is not None:
            total += acc[pl.ds(start, rows), :]
        out[pl.ds(start, rows), :] = total.astype(out.dtype)


def project_near_kernel(at, own_a, own_b, par_a, par_b, wa, wb, out):
    project_rows(at, (own_a, own_b), (par_a, par_b), (wa, wb), None, out)


def project_far_kernel(at, own_a, own_b, par_a, par_b, *rest):
    quarters, (acc, out, wa, wb) = rest[:RING], rest[RING:]
    rows = quarters[0].shape[0] // 2
    for i, quarter in enumerate(quarters):
        place = pl.ds(pl.multiple_of(at[3 + i] * rows, rows), rows)
        wa[place, :] = quarter[:rows, :]
        wb[place, :] = quarter[rows:, :]
    project_rows(at, (own_a, own_b), (par_a, par_b), (wa, wb), acc, out)


def project(scalars, hidden, partner, weights, acc):
    rows, depth, width = hidden.shape[0], hidden.shape[1] // N_FSDP, CHUNK_HEADS * 2 * HD
    far = acc is not None
    whole = lambda i, at: (0, 0)
    first = lambda i, at: (0, at[1])
    second = lambda i, at: (0, at[2])
    in_specs = [pl.BlockSpec((rows, depth), m) for m in (first, second, first, second)]
    in_specs += [pl.BlockSpec(w.shape, whole) for w in weights]
    args = [jnp.stack(scalars), hidden, hidden, partner, partner, *weights]
    if far:
        in_specs.append(pl.BlockSpec((2 * rows, width), whole))
        args.append(acc)
    return pl.pallas_call(
        project_far_kernel if far else project_near_kernel,
        out_shape=jax.ShapeDtypeStruct((2 * rows, width), jnp.bfloat16 if far else jnp.float32),
        grid_spec=pltpu.PrefetchScalarGridSpec(
            num_scalar_prefetch=1,
            grid=(1,),
            in_specs=in_specs,
            out_specs=pl.BlockSpec((2 * rows, width), whole),
            scratch_shapes=[pltpu.VMEM((depth, width), jnp.bfloat16)] * 2 if far else [],
        ),
        compiler_params=pltpu.CompilerParams(vmem_limit_bytes=40 * 1024 * 1024),
        cost_estimate=pl.CostEstimate(
            flops=8 * rows * depth * width, bytes_accessed=8 * rows * depth + 4 * depth * width, transcendentals=0
        ),
        name="project_far" if far else "project_near",
    )(*args)


def attend_kernel(at, q_own, q_par, query_doc, last_key, key_doc, *rest):
    windows, (out_own, out_par, keys, values, scores, sems) = rest[: SPAN + 1], rest[SPAN + 1 :]
    tile = pl.program_id(0)
    tiles = pl.num_programs(0)
    block_rows = windows[0].shape[0]
    width = CHUNK_HEADS * HD

    @pl.when(tile == 0)
    def _():
        copies = []
        for back in range(SPAN + 1):
            place = pl.ds((SPAN - back) * block_rows, block_rows)
            for part, held in enumerate((keys, values)):
                copies.append(
                    pltpu.make_async_copy(
                        windows[back].at[:, pl.ds(part * width, width)], held.at[place, :], sems.at[len(copies)]
                    )
                )
        for copy in copies:
            copy.start()
        for copy in copies:
            copy.wait()

    first, end = at[tile], at[tiles + tile]
    factor = math.log2(math.e) / math.sqrt(HD)
    for head in range(CHUNK_HEADS):
        lanes = slice(head * HD, (head + 1) * HD)

        def score(block, peaks):
            start = pl.multiple_of(block * TK, TK)
            place = pl.ds(start, TK)
            key = keys[place, lanes]
            position = start + lax.broadcasted_iota(jnp.int32, (TQ, TK), 1)
            allowed = jnp.logical_and(query_doc[...] == key_doc[:, place], position <= last_key[...])
            found = []
            for i in range(GROUP):
                columns = slice((head * GROUP + i) * HD, (head * GROUP + i + 1) * HD)
                query = jnp.where(tile < tiles // 2, q_own[:, columns], q_par[:, columns])
                s = lax.dot_general(query, key, (((1,), (1,)), ((), ())), preferred_element_type=jnp.float32)
                s = jnp.where(allowed, s, NEG)
                scores[i * TQ : (i + 1) * TQ, place] = s
                peak = peaks[i]
                for lane in range(0, TK, HD):
                    peak = jnp.maximum(peak, s[:, lane : lane + HD])
                found.append(peak)
            return tuple(found)

        start_peaks = tuple(jnp.full((TQ, HD), NEG, jnp.float32) for _ in range(GROUP))
        peaks = lax.fori_loop(first, end, score, start_peaks)
        highest = [jnp.max(peak, axis=1, keepdims=True) for peak in peaks]

        def weigh(block, carry):
            start = pl.multiple_of(block * TK, TK)
            place = pl.ds(start, TK)
            value = values[place, lanes]
            found = []
            for i in range(GROUP):
                total, summed = carry[i]
                w = jnp.exp2((scores[i * TQ : (i + 1) * TQ, place] - highest[i]) * factor)
                for lane in range(0, TK, HD):
                    total = total + w[:, lane : lane + HD]
                summed = summed + jnp.dot(w.astype(jnp.bfloat16), value, preferred_element_type=jnp.float32)
                found.append((total, summed))
            return tuple(found)

        zero = jnp.zeros((TQ, HD), jnp.float32)
        sums = lax.fori_loop(first, end, weigh, tuple((zero, zero) for _ in range(GROUP)))
        for i in range(GROUP):
            columns = slice((head * GROUP + i) * HD, (head * GROUP + i + 1) * HD)
            total, summed = sums[i]
            result = (summed / jnp.sum(total, axis=1, keepdims=True)).astype(jnp.bfloat16)

            @pl.when(tile < tiles // 2)
            def _():
                out_own[:, columns] = result

            @pl.when(tile >= tiles // 2)
            def _():
                out_par[:, columns] = result


def attend(at, q_own, q_par, query_doc, last_key, key_doc, windows, chunk):
    rows = q_own.shape[0]
    block_rows = windows[0].shape[0]
    n_keys = (SPAN + 1) * block_rows
    tiles = 2 * rows // TQ
    half = tiles // 2
    width = CHUNK_HEADS * GROUP * HD
    own = lambda i, at: (jnp.minimum(i, half - 1), 0)
    par = lambda i, at: (jnp.maximum(i - half, 0), 0)
    own_q = lambda i, at: (jnp.minimum(i, half - 1), chunk)
    par_q = lambda i, at: (jnp.maximum(i - half, 0), chunk)
    shape = jax.ShapeDtypeStruct((rows, width), jnp.bfloat16)
    return pl.pallas_call(
        attend_kernel,
        out_shape=[shape, shape],
        grid_spec=pltpu.PrefetchScalarGridSpec(
            num_scalar_prefetch=1,
            grid=(tiles,),
            in_specs=[
                pl.BlockSpec((TQ, width), own_q),
                pl.BlockSpec((TQ, width), par_q),
                pl.BlockSpec((TQ, 1), lambda i, at: (i, 0)),
                pl.BlockSpec((TQ, 1), lambda i, at: (i, 0)),
                pl.BlockSpec((1, n_keys), lambda i, at: (0, 0)),
            ]
            + [pl.BlockSpec(memory_space=pl.ANY)] * (SPAN + 1),
            out_specs=[pl.BlockSpec((TQ, width), own), pl.BlockSpec((TQ, width), par)],
            scratch_shapes=[
                pltpu.VMEM((n_keys, CHUNK_HEADS * HD), jnp.bfloat16),
                pltpu.VMEM((n_keys, CHUNK_HEADS * HD), jnp.bfloat16),
                pltpu.VMEM((GROUP * TQ, n_keys), jnp.float32),
                pltpu.SemaphoreType.DMA((2 * (SPAN + 1),)),
            ],
        ),
        compiler_params=pltpu.CompilerParams(vmem_limit_bytes=40 * 1024 * 1024),
        cost_estimate=pl.CostEstimate(
            flops=4 * 2 * rows * width * n_keys // 2, bytes_accessed=4 * n_keys * HD * CHUNK_HEADS, transcendentals=0
        ),
        name="attend",
    )(at, q_own, q_par, query_doc, last_key, key_doc, *windows)


def local(hidden, queries, kv_weights, image_groups, doc_ids):
    rows = hidden.shape[0]
    n_seq = lax.axis_size("seq")
    block_rows = rows * N_FSDP
    n_keys = (SPAN + 1) * block_rows
    seq_place = lax.axis_index("seq")
    fsdp_place = lax.axis_index("fsdp")
    core = fsdp_place % 2
    chip = fsdp_place // 2
    modality = image_groups[0]

    quarter = seq_place // (n_seq // RING)
    ring_modality = [modality] + [along_x(image_groups, -d, n_seq)[0] for d in range(1, RING)]
    fetched = pick_quarter(core, quarter, kv_weights)
    from_z, from_diagonal = [], []
    for j in range(CHUNKS):
        to_z, to_diagonal = fetched[2 * j], fetched[2 * j + 1]
        if j:
            to_z, to_diagonal, from_z[-1], from_diagonal[-1] = lax.optimization_barrier(
                (to_z, to_diagonal, from_z[-1], from_diagonal[-1])
            )
        from_z.append(swap(to_z, 2, n_seq))
        from_diagonal.append(swap(to_diagonal, 3, n_seq))
    picked = [w[0] for w in pick_own(core, modality, kv_weights)]
    mine, other = picked[0::2], picked[1::2]
    partner = swap(hidden, 1, n_seq)
    from_core = [swap(other[j], 1, n_seq) for j in range(CHUNKS)]
    half_heads = QH // 2 * HD
    q_own = lax.dynamic_slice_in_dim(queries, core * half_heads, half_heads, 1)
    q_par = swap(lax.dynamic_slice_in_dim(queries, (1 - core) * half_heads, half_heads, 1), 1, n_seq)

    padded = jnp.concatenate([jnp.full((SPAN * block_rows,), -1, jnp.int32), doc_ids])
    key_doc = lax.dynamic_slice_in_dim(padded, seq_place * block_rows, n_keys, 0)
    own_start = SPAN * block_rows + fsdp_place * rows
    par_start = SPAN * block_rows + (fsdp_place ^ 1) * rows
    starts = (own_start, par_start)
    query_doc = jnp.concatenate([lax.dynamic_slice_in_dim(key_doc, s, rows, 0) for s in starts])
    position = jnp.concatenate([s + jnp.arange(rows, dtype=jnp.int32) for s in starts])
    last_key = jnp.where(modality == 1, n_keys - 1, position)
    lowest = query_doc[::TQ]
    top = query_doc[TQ - 1 :: TQ]
    first = jnp.sum(key_doc[None, :] < lowest[:, None], axis=1) // TK
    doc_end = jnp.sum(key_doc[None, :] <= top[:, None], axis=1) - 1
    end = jnp.minimum(last_key[TQ - 1 :: TQ], doc_end) // TK + 1
    at = jnp.concatenate([first, end]).astype(jnp.int32)

    own_out, sent_out = [], []
    for j in range(CHUNKS):
        acc = project([core, fsdp_place, fsdp_place ^ 1], hidden, partner, [mine[j], from_core[j]], None)
        sent = pieces(jnp.stack(ring_modality), from_z[j], from_diagonal[j])
        quarters = [sent[0]] + [along_x(sent[d], d, n_seq) for d in range(1, RING)]
        places = [(quarter + RING - d) % RING for d in range(RING)]
        kv = project([core, fsdp_place ^ 2, fsdp_place ^ 3] + places, hidden, partner, quarters, acc)
        across = swap(kv, 2, n_seq)
        block_kv = jnp.where(chip == 0, jnp.concatenate([kv, across]), jnp.concatenate([across, kv]))
        windows = [block_kv] + [from_behind(block_kv, d, n_seq) for d in range(1, SPAN + 1)]
        out_own, out_par = attend(at, q_own, q_par, query_doc[:, None], last_key[:, None], key_doc[None, :], windows, j)
        own_out.append(out_own)
        sent_out.append(swap(out_par, 1, n_seq))
    own_out, sent_out = jnp.concatenate(own_out, 1), jnp.concatenate(sent_out, 1)
    return jnp.where(
        core == 0, jnp.concatenate([own_out, sent_out], 1), jnp.concatenate([sent_out, own_out], 1)
    )


def solution(mesh):
    in_specs = (
        P(("seq", "fsdp"), None),
        P(("seq", "fsdp"), None),
        P(None, "fsdp", None),
        P("seq"),
        P(),
    )
    out_specs = P(("seq", "fsdp"), None)
    return jax.shard_map(local, mesh=mesh, in_specs=in_specs, out_specs=out_specs, check_vma=False)
```

```python
import functools
import math

import jax
import jax.numpy as jnp
from jax import lax
from jax.experimental import pallas as pl
from jax.experimental.pallas import tpu as pltpu
from jax.sharding import PartitionSpec as P

KVH = 4
HD = 128
QH = 16
SPAN = 3
N_FSDP = 4
GROUP = QH // KVH
CORE_HEADS = KVH // 2
CHUNKS = 2
CHUNK_HEADS = CORE_HEADS // CHUNKS
RING = 4
TQ = 256
TK = 512
SUB = 128
FLAT = ("seq", "fsdp")
NEG = -1e30


def swap(block, bits, n_seq):
    route = [(s * N_FSDP + f, s * N_FSDP + (f ^ bits)) for s in range(n_seq) for f in range(N_FSDP)]
    return lax.ppermute(block, FLAT, route)


def next_row(block, n_seq):
    route = []
    for s in range(n_seq - RING):
        for f in range(N_FSDP):
            over = (s // RING) % RING == RING - 1
            route.append((s * N_FSDP + f, (s + RING) * N_FSDP + (f ^ 2 if over else f)))
    return lax.ppermute(block, FLAT, route)


def along_y(block, distance, n_seq):
    route = [
        (s * N_FSDP + f, (s // RING * RING + (s + distance) % RING) * N_FSDP + f)
        for s in range(n_seq)
        for f in range(N_FSDP)
    ]
    return lax.ppermute(block, FLAT, route)


def along_x(block, distance, n_seq):
    step = n_seq // RING
    route = [
        (s * N_FSDP + f, (s + distance * step) % n_seq * N_FSDP + f)
        for s in range(n_seq)
        for f in range(N_FSDP)
    ]
    return lax.ppermute(block, FLAT, route)


def cheap():
    return pl.CostEstimate(flops=1, bytes_accessed=1, transcendentals=0)


def pick_columns(core, chunk, part):
    width = CHUNK_HEADS * HD
    column = part * KVH * HD + core * (CORE_HEADS * HD) + chunk * width
    return pl.ds(pl.multiple_of(column, 128), width)


def pick_kernel(at, w_ref, *outs):
    width = CHUNK_HEADS * HD
    for side, out in enumerate(outs):
        core = at[0] if side == 0 else 1 - at[0]
        for chunk in range(CHUNKS):
            for part in range(2):
                place = (chunk * 2 + part) * width
                out[:, :, place : place + width] = w_ref[:, :, pick_columns(core, chunk, part)]


def pick(core, block, kv_weights, far):
    rows = kv_weights.shape[1] // RING
    heads = 2 if far else 1
    width = CORE_HEADS * 2 * HD
    if far:
        maps = (lambda i, at: (0, at[1], 0)), (lambda i, at: (0, 0, 0))
    else:
        maps = (lambda i, at: (at[1], i, 0)), (lambda i, at: (0, i, 0))
    shape = jax.ShapeDtypeStruct((heads, rows if far else RING * rows, width), jnp.bfloat16)
    return pl.pallas_call(
        pick_kernel,
        out_shape=[shape] * 2,
        grid_spec=pltpu.PrefetchScalarGridSpec(
            num_scalar_prefetch=1,
            grid=(1 if far else RING,),
            in_specs=[pl.BlockSpec((heads, rows, kv_weights.shape[2]), maps[0])],
            out_specs=[pl.BlockSpec((heads, rows, width), maps[1])] * 2,
        ),
        compiler_params=pltpu.CompilerParams(vmem_limit_bytes=60 * 1024 * 1024),
        cost_estimate=cheap(),
        name="pick_far" if far else "pick_near",
    )(jnp.stack([core, block]), kv_weights)


def piece_kernel(at, z_ref, d_ref, *outs):
    rows = z_ref.shape[1]
    for i, out in enumerate(outs):
        out[:rows, :] = z_ref[at[i]]
        out[rows:, :] = d_ref[at[i]]


def pieces(modalities, from_z, from_diagonal):
    shape = (2 * from_z.shape[1], from_z.shape[2])
    return pl.pallas_call(
        piece_kernel,
        out_shape=[jax.ShapeDtypeStruct(shape, jnp.bfloat16)] * RING,
        grid_spec=pltpu.PrefetchScalarGridSpec(
            num_scalar_prefetch=1,
            grid=(1,),
            in_specs=[pl.BlockSpec(from_z.shape, lambda i, at: (0, 0, 0))] * 2,
            out_specs=[pl.BlockSpec(shape, lambda i, at: (0, 0))] * RING,
        ),
        compiler_params=pltpu.CompilerParams(vmem_limit_bytes=60 * 1024 * 1024),
        cost_estimate=cheap(),
        name="pieces",
    )(modalities, from_z, from_diagonal)


def project_kernel(at, own, par, near, far, *rest):
    pieces_of, rest = rest[:RING], rest[RING:]
    outs, (wz, wd) = rest[:CHUNKS], rest[CHUNKS:]
    rows, quarter_rows = own.shape[0], pieces_of[0].shape[0] // 2
    depth, width = wz.shape[0], outs[0].shape[1]
    for i, piece in enumerate(pieces_of):
        place = pl.ds(pl.multiple_of(at[4 + i] * quarter_rows, quarter_rows), quarter_rows)
        wz[place, :] = piece[:quarter_rows, :]
        wd[place, :] = piece[quarter_rows:, :]
    for mine, x in enumerate((par, own)):
        start = pl.multiple_of((at[0] % 2 if mine else 1 - at[0] % 2) * rows, rows)
        total = jnp.zeros((rows, CHUNKS * width), jnp.float32)
        for i, w in enumerate((near, far, wz, wd)):
            columns = pl.ds(pl.multiple_of(at[i] * depth, 128), depth)
            total += jnp.dot(x[:, columns], w[...], preferred_element_type=jnp.float32)
        for chunk, out in enumerate(outs):
            out[pl.ds(start, rows), :] = total[:, chunk * width : (chunk + 1) * width].astype(out.dtype)


def project(scalars, hidden, partner, near, far, quarters):
    rows, depth, width = hidden.shape[0], hidden.shape[1] // N_FSDP, CHUNK_HEADS * 2 * HD
    whole = lambda i, at: (0, 0)
    args = [hidden, partner, near, far, *quarters]
    out = jax.ShapeDtypeStruct((2 * rows, width), jnp.bfloat16)
    return pl.pallas_call(
        project_kernel,
        out_shape=[out] * CHUNKS,
        grid_spec=pltpu.PrefetchScalarGridSpec(
            num_scalar_prefetch=1,
            grid=(1,),
            in_specs=[pl.BlockSpec(x.shape, whole) for x in args],
            out_specs=[pl.BlockSpec(out.shape, whole)] * CHUNKS,
            scratch_shapes=[pltpu.VMEM((depth, CHUNKS * width), jnp.bfloat16)] * 2,
        ),
        compiler_params=pltpu.CompilerParams(vmem_limit_bytes=60 * 1024 * 1024),
        cost_estimate=cheap(),
        name="project",
    )(jnp.stack(scalars), *args)


def attend_kernel(at, q_own, q_par, query_doc, last_key, key_doc, *rest):
    windows, rest = rest[: SPAN + 1], rest[SPAN + 1 :]
    out_own, out_par, keys, values, turned, scores, stacked, sems = rest
    tile = pl.program_id(0)
    tiles = pl.num_programs(0)
    block_rows = windows[0].shape[0]
    width = CHUNK_HEADS * HD

    @pl.when(tile == 0)
    def _():
        copies = []
        for back in range(SPAN + 1):
            place = pl.ds((SPAN - back) * block_rows, block_rows)
            for part, held in enumerate((keys, values)):
                copies.append(
                    pltpu.make_async_copy(
                        windows[back].at[:, pl.ds(part * width, width)], held.at[place, :], sems.at[len(copies)]
                    )
                )
        for copy in copies:
            copy.start()
        for copy in copies:
            copy.wait()

        low, high = at[0], at[tiles]
        for i in range(1, tiles):
            low, high = jnp.minimum(low, at[i]), jnp.maximum(high, at[tiles + i])

        def turn(block, carry):
            place = pl.ds(pl.multiple_of(block * TK, TK), TK)
            turned[:, place] = values[place, :].T
            return carry

        lax.fori_loop(low, high, turn, 0)

    first, end = at[tile], at[tiles + tile]
    factor = math.log2(math.e) / math.sqrt(HD)
    rows = GROUP * TQ
    for head in range(CHUNK_HEADS):
        lanes = slice(head * HD, (head + 1) * HD)

        def gather(ref):
            for i in range(GROUP):
                columns = slice((head * GROUP + i) * HD, (head * GROUP + i + 1) * HD)
                stacked[:, i * TQ : (i + 1) * TQ] = ref[:, columns].T

        pl.when(tile < tiles // 2)(lambda: gather(q_own))
        pl.when(tile >= tiles // 2)(lambda: gather(q_par))

        def score(block, peak):
            start = pl.multiple_of(block * TK, TK)
            s = jnp.dot(keys[pl.ds(start, TK), lanes], stacked[...], preferred_element_type=jnp.float32)
            for row in range(0, TK, SUB):
                span = pl.ds(pl.multiple_of(start + row, SUB), SUB)
                position = start + row + lax.broadcasted_iota(jnp.int32, (SUB, TQ), 0)
                docs = jnp.broadcast_to(key_doc[span, :], (SUB, TQ))
                allowed = jnp.logical_and(docs == query_doc[...], position <= last_key[...])
                found = []
                for i in range(GROUP):
                    part = jnp.where(allowed, s[row : row + SUB, i * TQ : (i + 1) * TQ], NEG)
                    scores[span, i * TQ : (i + 1) * TQ] = part
                    found.append(jnp.max(part.reshape(SUB // 8, 8, TQ), axis=0))
                peak = jnp.maximum(peak, jnp.concatenate(found, axis=1))
            return peak

        peak = lax.fori_loop(first, end, score, jnp.full((8, rows), NEG, jnp.float32))
        highest = jnp.max(peak, axis=0, keepdims=True) * factor

        def weigh(block, carry):
            total, summed = carry
            start = pl.multiple_of(block * TK, TK)
            weights = []
            for row in range(0, TK, SUB):
                span = pl.ds(pl.multiple_of(start + row, SUB), SUB)
                w = jnp.exp2(scores[span, :] * factor - highest)
                total = total + jnp.sum(w.reshape(SUB // 8, 8, rows), axis=0)
                weights.append(w.astype(jnp.bfloat16))
            value = turned[lanes, pl.ds(start, TK)]
            summed = summed + jnp.dot(
                value, jnp.concatenate(weights, axis=0), preferred_element_type=jnp.float32
            )
            return total, summed

        zero = (jnp.zeros((8, rows), jnp.float32), jnp.zeros((HD, rows), jnp.float32))
        total, summed = lax.fori_loop(first, end, weigh, zero)
        result = summed / jnp.sum(total, axis=0, keepdims=True)

        def put(ref):
            for i in range(GROUP):
                columns = slice((head * GROUP + i) * HD, (head * GROUP + i + 1) * HD)
                ref[:, columns] = result[:, i * TQ : (i + 1) * TQ].T.astype(jnp.bfloat16)

        pl.when(tile < tiles // 2)(lambda: put(out_own))
        pl.when(tile >= tiles // 2)(lambda: put(out_par))


def attend(at, q_own, q_par, query_doc, last_key, key_doc, windows, chunk):
    rows = q_own.shape[0]
    block_rows = windows[0].shape[0]
    n_keys = (SPAN + 1) * block_rows
    tiles = 2 * rows // TQ
    half = tiles // 2
    width = CHUNK_HEADS * GROUP * HD
    own = lambda i, at: (jnp.minimum(i, half - 1), 0)
    par = lambda i, at: (jnp.maximum(i - half, 0), 0)
    own_q = lambda i, at: (jnp.minimum(i, half - 1), chunk)
    par_q = lambda i, at: (jnp.maximum(i - half, 0), chunk)
    shape = jax.ShapeDtypeStruct((rows, width), jnp.bfloat16)
    return pl.pallas_call(
        attend_kernel,
        out_shape=[shape, shape],
        grid_spec=pltpu.PrefetchScalarGridSpec(
            num_scalar_prefetch=1,
            grid=(tiles,),
            in_specs=[
                pl.BlockSpec((TQ, width), own_q),
                pl.BlockSpec((TQ, width), par_q),
                pl.BlockSpec((1, TQ), lambda i, at: (0, i)),
                pl.BlockSpec((1, TQ), lambda i, at: (0, i)),
                pl.BlockSpec((n_keys, 1), lambda i, at: (0, 0)),
            ]
            + [pl.BlockSpec(memory_space=pl.ANY)] * (SPAN + 1),
            out_specs=[pl.BlockSpec((TQ, width), own), pl.BlockSpec((TQ, width), par)],
            scratch_shapes=[
                pltpu.VMEM((n_keys, CHUNK_HEADS * HD), jnp.bfloat16),
                pltpu.VMEM((n_keys, CHUNK_HEADS * HD), jnp.bfloat16),
                pltpu.VMEM((CHUNK_HEADS * HD, n_keys), jnp.bfloat16),
                pltpu.VMEM((n_keys, GROUP * TQ), jnp.float32),
                pltpu.VMEM((HD, GROUP * TQ), jnp.bfloat16),
                pltpu.SemaphoreType.DMA((2 * (SPAN + 1),)),
            ],
        ),
        compiler_params=pltpu.CompilerParams(vmem_limit_bytes=40 * 1024 * 1024),
        cost_estimate=cheap(),
        name="attend",
    )(at, q_own, q_par, query_doc, last_key, key_doc, *windows)


def local(hidden, queries, kv_weights, image_groups, doc_ids):
    rows = hidden.shape[0]
    n_seq = lax.axis_size("seq")
    block_rows = rows * N_FSDP
    n_keys = (SPAN + 1) * block_rows
    seq_place = lax.axis_index("seq")
    fsdp_place = lax.axis_index("fsdp")
    core = fsdp_place % 2
    chip = fsdp_place // 2
    modality = image_groups[0]

    quarter = seq_place // (n_seq // RING)
    fetched = pick(core, quarter, kv_weights, True)
    fetched, kv_weights, image_groups = lax.optimization_barrier((fetched, kv_weights, image_groups))
    from_z, from_diagonal = swap(fetched[0], 2, n_seq), swap(fetched[1], 3, n_seq)
    ring_modality = [modality] + [along_x(image_groups, -d, n_seq)[0] for d in range(1, RING)]
    mine, other = [w[0] for w in pick(core, modality, kv_weights, False)]
    partner = swap(hidden, 1, n_seq)
    from_core = swap(other, 1, n_seq)
    half_heads = QH // 2 * HD
    q_own = lax.dynamic_slice_in_dim(queries, core * half_heads, half_heads, 1)
    q_par = swap(lax.dynamic_slice_in_dim(queries, (1 - core) * half_heads, half_heads, 1), 1, n_seq)

    from_z, from_diagonal, mine = lax.optimization_barrier((from_z, from_diagonal, mine))
    sent = pieces(jnp.stack(ring_modality), from_z, from_diagonal)
    quarters = [sent[0]] + [along_x(sent[d], d, n_seq) for d in range(1, RING)]
    places = [(quarter + RING - d) % RING for d in range(RING)]
    fsdp_order = [fsdp_place ^ bits for bits in range(N_FSDP)]
    kv = project(fsdp_order + places, hidden, partner, mine, from_core, quarters)
    kv, doc_ids = lax.optimization_barrier((kv, doc_ids))
    padded = jnp.concatenate([jnp.full((SPAN * block_rows,), -1, jnp.int32), doc_ids])
    key_doc = lax.dynamic_slice_in_dim(padded, seq_place * block_rows, n_keys, 0)
    own_start = SPAN * block_rows + fsdp_place * rows
    par_start = SPAN * block_rows + (fsdp_place ^ 1) * rows
    starts = (own_start, par_start)
    query_doc = jnp.concatenate([lax.dynamic_slice_in_dim(key_doc, s, rows, 0) for s in starts])
    position = jnp.concatenate([s + jnp.arange(rows, dtype=jnp.int32) for s in starts])
    last_key = jnp.where(modality == 1, n_keys - 1, position)
    lowest = query_doc[::TQ]
    top = query_doc[TQ - 1 :: TQ]
    first = jnp.sum(key_doc[None, :] < lowest[:, None], axis=1) // TK
    doc_end = jnp.sum(key_doc[None, :] <= top[:, None], axis=1) - 1
    end = jnp.minimum(last_key[TQ - 1 :: TQ], doc_end) // TK + 1
    at = jnp.concatenate([first, end]).astype(jnp.int32)

    row_place = seq_place % RING
    across = [swap(x, 2, n_seq) for x in kv]
    across, at, query_doc, last_key, key_doc = lax.optimization_barrier((across, at, query_doc, last_key, key_doc))
    block_kv = [
        jnp.where(chip == 0, jnp.concatenate([x, y]), jnp.concatenate([y, x])) for x, y in zip(kv, across)
    ]
    before = [next_row(x, n_seq) for x in block_kv]
    before[0], block_kv = lax.optimization_barrier((before[0], block_kv))
    own_out, sent_out = [], []
    for j in range(CHUNKS):
        windows = [block_kv[j]] + [
            along_y(jnp.where(row_place + d < RING, block_kv[j], before[j]), d, n_seq) for d in range(1, SPAN + 1)
        ]
        out_own, out_par = attend(at, q_own, q_par, query_doc[None, :], last_key[None, :], key_doc[:, None], windows, j)
        own_out.append(out_own)
        sent_out.append(swap(out_par, 1, n_seq))
    own_out, sent_out = jnp.concatenate(own_out, 1), jnp.concatenate(sent_out, 1)
    return jnp.where(
        core == 0, jnp.concatenate([own_out, sent_out], 1), jnp.concatenate([sent_out, own_out], 1)
    )


def solution(mesh):
    in_specs = (
        P(("seq", "fsdp"), None),
        P(("seq", "fsdp"), None),
        P(None, "fsdp", None),
        P("seq"),
        P(),
    )
    out_specs = P(("seq", "fsdp"), None)
    return jax.shard_map(local, mesh=mesh, in_specs=in_specs, out_specs=out_specs, check_vma=False)
```

```python
import functools
import math

import jax
import jax.numpy as jnp
from jax import lax
from jax.experimental import pallas as pl
from jax.experimental.pallas import tpu as pltpu
from jax.sharding import PartitionSpec as P

KVH = 4
HD = 128
QH = 16
SPAN = 3
N_FSDP = 4
GROUP = QH // KVH
CORE_HEADS = KVH // 2
CHUNKS = 2
CHUNK_HEADS = CORE_HEADS // CHUNKS
RING = 4
TQ = 256
TK = 512
SUB = 128
FLAT = ("seq", "fsdp")
NEG = -1e30


def swap(block, bits, n_seq):
    route = [(s * N_FSDP + f, s * N_FSDP + (f ^ bits)) for s in range(n_seq) for f in range(N_FSDP)]
    return lax.ppermute(block, FLAT, route)


def from_behind(block, distance, n_seq):
    route = [
        (s * N_FSDP + f, (s + distance) * N_FSDP + f)
        for s in range(n_seq - distance)
        for f in range(N_FSDP)
    ]
    return lax.ppermute(block, FLAT, route)


def along_x(block, distance, n_seq):
    step = n_seq // RING
    route = [
        (s * N_FSDP + f, (s + distance * step) % n_seq * N_FSDP + f)
        for s in range(n_seq)
        for f in range(N_FSDP)
    ]
    return lax.ppermute(block, FLAT, route)


def pick_kernel(at, w_ref, *outs):
    width = CHUNK_HEADS * HD
    for i in range(2 * CHUNKS):
        core = at[0] if i % 2 == 0 else 1 - at[0]
        for part in range(2):
            column = part * KVH * HD + core * (CORE_HEADS * HD) + i // 2 * width
            columns = pl.ds(pl.multiple_of(column, 128), width)
            outs[i][:, :, part * width : (part + 1) * width] = w_ref[:, :, columns]


def pick_own(core, modality, kv_weights):
    depth = kv_weights.shape[1]
    rows = depth // RING
    shape = (1, depth, CHUNK_HEADS * 2 * HD)
    n = 2 * CHUNKS
    return pl.pallas_call(
        pick_kernel,
        out_shape=[jax.ShapeDtypeStruct(shape, jnp.bfloat16)] * n,
        grid_spec=pltpu.PrefetchScalarGridSpec(
            num_scalar_prefetch=1,
            grid=(RING,),
            in_specs=[pl.BlockSpec((1, rows, kv_weights.shape[2]), lambda i, at: (at[1], i, 0))],
            out_specs=[pl.BlockSpec((1, rows, shape[2]), lambda i, at: (0, i, 0))] * n,
        ),
        name="pick_own",
    )(jnp.stack([core, modality]), kv_weights)


def pick_quarter(core, quarter, kv_weights):
    rows = kv_weights.shape[1] // RING
    shape = (2, rows, CHUNK_HEADS * 2 * HD)
    n = 2 * CHUNKS
    return pl.pallas_call(
        pick_kernel,
        out_shape=[jax.ShapeDtypeStruct(shape, jnp.bfloat16)] * n,
        grid_spec=pltpu.PrefetchScalarGridSpec(
            num_scalar_prefetch=1,
            grid=(1,),
            in_specs=[pl.BlockSpec((2, rows, kv_weights.shape[2]), lambda i, at: (0, at[1], 0))],
            out_specs=[pl.BlockSpec(shape, lambda i, at: (0, 0, 0))] * n,
        ),
        name="pick_quarter",
    )(jnp.stack([core, quarter]), kv_weights)


def piece_kernel(at, z_ref, d_ref, *outs):
    rows = z_ref.shape[1]
    for i, out in enumerate(outs):
        out[:rows, :] = z_ref[at[i]]
        out[rows:, :] = d_ref[at[i]]


def pieces(modalities, from_z, from_diagonal):
    shape = (2 * from_z.shape[1], from_z.shape[2])
    return pl.pallas_call(
        piece_kernel,
        out_shape=[jax.ShapeDtypeStruct(shape, jnp.bfloat16)] * RING,
        grid_spec=pltpu.PrefetchScalarGridSpec(
            num_scalar_prefetch=1,
            grid=(1,),
            in_specs=[pl.BlockSpec(from_z.shape, lambda i, at: (0, 0, 0))] * 2,
            out_specs=[pl.BlockSpec(shape, lambda i, at: (0, 0))] * RING,
        ),
        name="pieces",
    )(modalities, from_z, from_diagonal)


def project_rows(at, own, par, weights, acc, out):
    rows = out.shape[0] // 2
    for mine, x in enumerate((par, own)):
        start = pl.multiple_of((at[0] if mine else 1 - at[0]) * rows, rows)
        total = jnp.dot(x[0][...], weights[0][...], preferred_element_type=jnp.float32)
        total += jnp.dot(x[1][...], weights[1][...], preferred_element_type=jnp.float32)
        if acc is not None:
            total += acc[pl.ds(start, rows), :]
        out[pl.ds(start, rows), :] = total.astype(out.dtype)


def project_near_kernel(at, own_a, own_b, par_a, par_b, wa, wb, out):
    project_rows(at, (own_a, own_b), (par_a, par_b), (wa, wb), None, out)


def project_far_kernel(at, own_a, own_b, par_a, par_b, *rest):
    quarters, (acc, out, wa, wb) = rest[:RING], rest[RING:]
    rows = quarters[0].shape[0] // 2
    for i, quarter in enumerate(quarters):
        place = pl.ds(pl.multiple_of(at[3 + i] * rows, rows), rows)
        wa[place, :] = quarter[:rows, :]
        wb[place, :] = quarter[rows:, :]
    project_rows(at, (own_a, own_b), (par_a, par_b), (wa, wb), acc, out)


def project(scalars, hidden, partner, weights, acc):
    rows, depth, width = hidden.shape[0], hidden.shape[1] // N_FSDP, CHUNK_HEADS * 2 * HD
    far = acc is not None
    whole = lambda i, at: (0, 0)
    first = lambda i, at: (0, at[1])
    second = lambda i, at: (0, at[2])
    in_specs = [pl.BlockSpec((rows, depth), m) for m in (first, second, first, second)]
    in_specs += [pl.BlockSpec(w.shape, whole) for w in weights]
    args = [jnp.stack(scalars), hidden, hidden, partner, partner, *weights]
    if far:
        in_specs.append(pl.BlockSpec((2 * rows, width), whole))
        args.append(acc)
    return pl.pallas_call(
        project_far_kernel if far else project_near_kernel,
        out_shape=jax.ShapeDtypeStruct((2 * rows, width), jnp.bfloat16 if far else jnp.float32),
        grid_spec=pltpu.PrefetchScalarGridSpec(
            num_scalar_prefetch=1,
            grid=(1,),
            in_specs=in_specs,
            out_specs=pl.BlockSpec((2 * rows, width), whole),
            scratch_shapes=[pltpu.VMEM((depth, width), jnp.bfloat16)] * 2 if far else [],
        ),
        compiler_params=pltpu.CompilerParams(vmem_limit_bytes=40 * 1024 * 1024),
        cost_estimate=pl.CostEstimate(
            flops=8 * rows * depth * width, bytes_accessed=8 * rows * depth + 4 * depth * width, transcendentals=0
        ),
        name="project_far" if far else "project_near",
    )(*args)


def attend_kernel(at, q_own, q_par, query_doc, last_key, key_doc, *rest):
    windows, rest = rest[: SPAN + 1], rest[SPAN + 1 :]
    out_own, out_par, keys, values, turned, scores, stacked, sems = rest
    tile = pl.program_id(0)
    tiles = pl.num_programs(0)
    block_rows = windows[0].shape[0]
    width = CHUNK_HEADS * HD

    @pl.when(tile == 0)
    def _():
        copies = []
        for back in range(SPAN + 1):
            place = pl.ds((SPAN - back) * block_rows, block_rows)
            for part, held in enumerate((keys, values)):
                copies.append(
                    pltpu.make_async_copy(
                        windows[back].at[:, pl.ds(part * width, width)], held.at[place, :], sems.at[len(copies)]
                    )
                )
        for copy in copies:
            copy.start()
        for copy in copies:
            copy.wait()

        low, high = at[0], at[tiles]
        for i in range(1, tiles):
            low, high = jnp.minimum(low, at[i]), jnp.maximum(high, at[tiles + i])

        def turn(block, carry):
            place = pl.ds(pl.multiple_of(block * TK, TK), TK)
            turned[:, place] = values[place, :].T
            return carry

        lax.fori_loop(low, high, turn, 0)

    first, end = at[tile], at[tiles + tile]
    factor = math.log2(math.e) / math.sqrt(HD)
    rows = GROUP * TQ
    for head in range(CHUNK_HEADS):
        lanes = slice(head * HD, (head + 1) * HD)

        def gather(ref):
            for i in range(GROUP):
                columns = slice((head * GROUP + i) * HD, (head * GROUP + i + 1) * HD)
                stacked[:, i * TQ : (i + 1) * TQ] = ref[:, columns].T

        pl.when(tile < tiles // 2)(lambda: gather(q_own))
        pl.when(tile >= tiles // 2)(lambda: gather(q_par))

        def score(block, peak):
            start = pl.multiple_of(block * TK, TK)
            s = jnp.dot(keys[pl.ds(start, TK), lanes], stacked[...], preferred_element_type=jnp.float32)
            for row in range(0, TK, SUB):
                span = pl.ds(pl.multiple_of(start + row, SUB), SUB)
                position = start + row + lax.broadcasted_iota(jnp.int32, (SUB, TQ), 0)
                docs = jnp.broadcast_to(key_doc[span, :], (SUB, TQ))
                allowed = jnp.logical_and(docs == query_doc[...], position <= last_key[...])
                found = []
                for i in range(GROUP):
                    part = jnp.where(allowed, s[row : row + SUB, i * TQ : (i + 1) * TQ], NEG)
                    scores[span, i * TQ : (i + 1) * TQ] = part
                    found.append(jnp.max(part.reshape(SUB // 8, 8, TQ), axis=0))
                peak = jnp.maximum(peak, jnp.concatenate(found, axis=1))
            return peak

        peak = lax.fori_loop(first, end, score, jnp.full((8, rows), NEG, jnp.float32))
        highest = jnp.max(peak, axis=0, keepdims=True) * factor

        def weigh(block, carry):
            total, summed = carry
            start = pl.multiple_of(block * TK, TK)
            weights = []
            for row in range(0, TK, SUB):
                span = pl.ds(pl.multiple_of(start + row, SUB), SUB)
                w = jnp.exp2(scores[span, :] * factor - highest)
                total = total + jnp.sum(w.reshape(SUB // 8, 8, rows), axis=0)
                weights.append(w.astype(jnp.bfloat16))
            value = turned[lanes, pl.ds(start, TK)]
            summed = summed + jnp.dot(
                value, jnp.concatenate(weights, axis=0), preferred_element_type=jnp.float32
            )
            return total, summed

        zero = (jnp.zeros((8, rows), jnp.float32), jnp.zeros((HD, rows), jnp.float32))
        total, summed = lax.fori_loop(first, end, weigh, zero)
        result = summed / jnp.sum(total, axis=0, keepdims=True)

        def put(ref):
            for i in range(GROUP):
                columns = slice((head * GROUP + i) * HD, (head * GROUP + i + 1) * HD)
                ref[:, columns] = result[:, i * TQ : (i + 1) * TQ].T.astype(jnp.bfloat16)

        pl.when(tile < tiles // 2)(lambda: put(out_own))
        pl.when(tile >= tiles // 2)(lambda: put(out_par))


def attend(at, q_own, q_par, query_doc, last_key, key_doc, windows, chunk):
    rows = q_own.shape[0]
    block_rows = windows[0].shape[0]
    n_keys = (SPAN + 1) * block_rows
    tiles = 2 * rows // TQ
    half = tiles // 2
    width = CHUNK_HEADS * GROUP * HD
    own = lambda i, at: (jnp.minimum(i, half - 1), 0)
    par = lambda i, at: (jnp.maximum(i - half, 0), 0)
    own_q = lambda i, at: (jnp.minimum(i, half - 1), chunk)
    par_q = lambda i, at: (jnp.maximum(i - half, 0), chunk)
    shape = jax.ShapeDtypeStruct((rows, width), jnp.bfloat16)
    return pl.pallas_call(
        attend_kernel,
        out_shape=[shape, shape],
        grid_spec=pltpu.PrefetchScalarGridSpec(
            num_scalar_prefetch=1,
            grid=(tiles,),
            in_specs=[
                pl.BlockSpec((TQ, width), own_q),
                pl.BlockSpec((TQ, width), par_q),
                pl.BlockSpec((1, TQ), lambda i, at: (0, i)),
                pl.BlockSpec((1, TQ), lambda i, at: (0, i)),
                pl.BlockSpec((n_keys, 1), lambda i, at: (0, 0)),
            ]
            + [pl.BlockSpec(memory_space=pl.ANY)] * (SPAN + 1),
            out_specs=[pl.BlockSpec((TQ, width), own), pl.BlockSpec((TQ, width), par)],
            scratch_shapes=[
                pltpu.VMEM((n_keys, CHUNK_HEADS * HD), jnp.bfloat16),
                pltpu.VMEM((n_keys, CHUNK_HEADS * HD), jnp.bfloat16),
                pltpu.VMEM((CHUNK_HEADS * HD, n_keys), jnp.bfloat16),
                pltpu.VMEM((n_keys, GROUP * TQ), jnp.float32),
                pltpu.VMEM((HD, GROUP * TQ), jnp.bfloat16),
                pltpu.SemaphoreType.DMA((2 * (SPAN + 1),)),
            ],
        ),
        compiler_params=pltpu.CompilerParams(vmem_limit_bytes=40 * 1024 * 1024),
        cost_estimate=pl.CostEstimate(
            flops=4 * 2 * rows * width * n_keys // 2, bytes_accessed=4 * n_keys * HD * CHUNK_HEADS, transcendentals=0
        ),
        name="attend",
    )(at, q_own, q_par, query_doc, last_key, key_doc, *windows)


def local(hidden, queries, kv_weights, image_groups, doc_ids):
    rows = hidden.shape[0]
    n_seq = lax.axis_size("seq")
    block_rows = rows * N_FSDP
    n_keys = (SPAN + 1) * block_rows
    seq_place = lax.axis_index("seq")
    fsdp_place = lax.axis_index("fsdp")
    core = fsdp_place % 2
    chip = fsdp_place // 2
    modality = image_groups[0]

    quarter = seq_place // (n_seq // RING)
    ring_modality = [modality] + [along_x(image_groups, -d, n_seq)[0] for d in range(1, RING)]
    fetched = pick_quarter(core, quarter, kv_weights)
    from_z, from_diagonal = [], []
    for j in range(CHUNKS):
        to_z, to_diagonal = fetched[2 * j], fetched[2 * j + 1]
        if j:
            to_z, to_diagonal, from_z[-1], from_diagonal[-1] = lax.optimization_barrier(
                (to_z, to_diagonal, from_z[-1], from_diagonal[-1])
            )
        from_z.append(swap(to_z, 2, n_seq))
        from_diagonal.append(swap(to_diagonal, 3, n_seq))
    picked = [w[0] for w in pick_own(core, modality, kv_weights)]
    mine, other = picked[0::2], picked[1::2]
    partner = swap(hidden, 1, n_seq)
    from_core = [swap(other[j], 1, n_seq) for j in range(CHUNKS)]
    half_heads = QH // 2 * HD
    q_own = lax.dynamic_slice_in_dim(queries, core * half_heads, half_heads, 1)
    q_par = swap(lax.dynamic_slice_in_dim(queries, (1 - core) * half_heads, half_heads, 1), 1, n_seq)

    padded = jnp.concatenate([jnp.full((SPAN * block_rows,), -1, jnp.int32), doc_ids])
    key_doc = lax.dynamic_slice_in_dim(padded, seq_place * block_rows, n_keys, 0)
    own_start = SPAN * block_rows + fsdp_place * rows
    par_start = SPAN * block_rows + (fsdp_place ^ 1) * rows
    starts = (own_start, par_start)
    query_doc = jnp.concatenate([lax.dynamic_slice_in_dim(key_doc, s, rows, 0) for s in starts])
    position = jnp.concatenate([s + jnp.arange(rows, dtype=jnp.int32) for s in starts])
    last_key = jnp.where(modality == 1, n_keys - 1, position)
    lowest = query_doc[::TQ]
    top = query_doc[TQ - 1 :: TQ]
    first = jnp.sum(key_doc[None, :] < lowest[:, None], axis=1) // TK
    doc_end = jnp.sum(key_doc[None, :] <= top[:, None], axis=1) - 1
    end = jnp.minimum(last_key[TQ - 1 :: TQ], doc_end) // TK + 1
    at = jnp.concatenate([first, end]).astype(jnp.int32)

    own_out, sent_out = [], []
    for j in range(CHUNKS):
        acc = project([core, fsdp_place, fsdp_place ^ 1], hidden, partner, [mine[j], from_core[j]], None)
        sent = pieces(jnp.stack(ring_modality), from_z[j], from_diagonal[j])
        quarters = [sent[0]] + [along_x(sent[d], d, n_seq) for d in range(1, RING)]
        places = [(quarter + RING - d) % RING for d in range(RING)]
        kv = project([core, fsdp_place ^ 2, fsdp_place ^ 3] + places, hidden, partner, quarters, acc)
        across = swap(kv, 2, n_seq)
        block_kv = jnp.where(chip == 0, jnp.concatenate([kv, across]), jnp.concatenate([across, kv]))
        windows = [block_kv] + [from_behind(block_kv, d, n_seq) for d in range(1, SPAN + 1)]
        out_own, out_par = attend(at, q_own, q_par, query_doc[None, :], last_key[None, :], key_doc[:, None], windows, j)
        own_out.append(out_own)
        sent_out.append(swap(out_par, 1, n_seq))
    own_out, sent_out = jnp.concatenate(own_out, 1), jnp.concatenate(sent_out, 1)
    return jnp.where(
        core == 0, jnp.concatenate([own_out, sent_out], 1), jnp.concatenate([sent_out, own_out], 1)
    )


def solution(mesh):
    in_specs = (
        P(("seq", "fsdp"), None),
        P(("seq", "fsdp"), None),
        P(None, "fsdp", None),
        P("seq"),
        P(),
    )
    out_specs = P(("seq", "fsdp"), None)
    return jax.shard_map(local, mesh=mesh, in_specs=in_specs, out_specs=out_specs, check_vma=False)
```
